256 devices in a mesh: row: 8 (over y, core), col: 8 (over z), layer: 4 (over x).
Axes of the slice: x: 4, y: 4, z: 8, core: 2. Of those that a mesh axis runs over, the one named last changes fastest.
Arguments:
- a_blocks: bfloat16 [1536, 128, 128], P(('row', 'col', 'layer')), may hold values from -6 to 6
- a_where: int32 [1536, 2], P(('row', 'col', 'layer')), may hold values from 0 to 63, as said below
- b_blocks: bfloat16 [2048, 128, 128], P(('row', 'col', 'layer')), may hold values from -0.375 to 0.375
- b_where: int32 [2048, 2], P(('row', 'col', 'layer')), may hold values from 0 to 63, as said below
Outputs:
- product: float32 [16384, 16384], P('row', ('col', 'layer'))
The draws below stay inside these ranges and needn't reach their ends.
Inputs may be any that keep to these rules, and one draw needn't show every extreme that they name: For slot s on the device with grid coordinates (p, q, t): a_where[s, 1] = (m * (number of col devices) + q) * (number of layer devices) + t for some m below 2; a_where[s, 0] is a block row below 16, or 16 for an empty slot. No device holds the same (row, column) pair twice. At least a quarter of each device's slots are live, at positions drawn from the seed, and in every draw some device has all 6 slots live. For slot s on the device with grid coordinates (p, q, t): b_where[s, 0] is a block row k of B with k mod (number of row devices) = p; b_where[s, 1] is a local block column below 4, or 4 for an empty slot. No device holds the same pair twice. At least a quarter of each device's slots are live, at positions drawn from the seed, and in every draw some device has all 8 slots live.
All inputs are finite; a program needn't handle non-finite values.
Results may differ from the reference program's by a relative error of at most 0.0003.
Values may be sent and summed in bfloat16 or wider, within the bound.
No kernel may reach another device: no remote copies, remote signals or barrier semaphores. Data moves between devices by JAX's collectives and lax.ppermute only.
A program may use at most 128 MiB of HBM per device.

```python
import jax
import jax.numpy as jnp
from jax import lax

BS = 128
RB = 16
CS = 4
KD = 2
SA = 6
SB = 8
DEVICES_ALL = 256
N_ROW = 8
N_COL = 8
N_LAYER = 4


def slot_layout(key, capacity, options, devices):
    keys = jax.random.split(key, devices)

    def one_device(sub):
        first, second, third = jax.random.split(sub, 3)
        picked = jax.random.permutation(first, options)[:capacity]
        order = jax.random.permutation(second, capacity)
        count = jax.random.randint(third, (), (capacity + 3) // 4, capacity + 1)
        return (picked, order, count)
    picked, order, count = jax.vmap(one_device)(keys)
    fullest = jax.random.randint(jax.random.fold_in(key, 99), (), 0, devices)
    count = jnp.where(jnp.arange(devices) == fullest, capacity, count)
    live = order < count[:, None]
    return (picked, live)


def draw_a_where(key, part):
    key = jax.random.fold_in(key, 11)
    devices = N_ROW * N_COL * N_LAYER
    picked, live = slot_layout(key, SA, RB * KD, devices)
    block_row = picked // KD
    inner = picked % KD
    device = jnp.arange(devices)
    col_pos = device // N_LAYER % N_COL
    layer_pos = device % N_LAYER
    column = (inner * N_COL + col_pos[:, None]) * N_LAYER + layer_pos[:, None]
    block_row = jnp.where(live, block_row, RB)
    return jnp.stack([block_row, column], -1).reshape(devices * SA, 2).astype(jnp.int32)


def draw_b_where(key, part):
    key = jax.random.fold_in(key, 23)
    devices = N_ROW * N_COL * N_LAYER
    per_row = KD * N_COL * N_LAYER // N_ROW
    picked, live = slot_layout(key, SB, per_row * CS, devices)
    device = jnp.arange(devices)
    row_pos = device // (N_COL * N_LAYER)
    block_row = picked // CS * N_ROW + row_pos[:, None]
    local_col = jnp.where(live, picked % CS, CS)
    return jnp.stack([block_row, local_col], -1).reshape(devices * SB, 2).astype(jnp.int32)


def block_levels(own_key, dims, cuts, least, largest):
    factor_of = 1.0
    for dim, shards_of in cuts:
        draws = jax.random.uniform(jax.random.fold_in(jax.random.fold_in(own_key, 6), dim), (shards_of,), jnp.float32, least / len(cuts), largest / len(cuts))
        factor_of = factor_of * jnp.repeat(jnp.exp(draws), dims[dim] // shards_of).reshape((-1,) + (1,) * (len(dims) - 1 - dim))
    return factor_of


def bell_draw(key, dims, deviation, reach, shards=(), held_as=jnp.bfloat16):
    drawn = deviation * jax.random.normal(key, dims, jnp.float32)
    if shards:
        drawn = drawn * block_levels(key, dims, shards, -0.22, 0.18)
    return jnp.clip(drawn, -reach, reach).astype(held_as)


def setup_inputs(seed: int = 0) -> dict:
    arg_keys = jax.random.split(jax.random.key(seed), 5)
    a_blocks = bell_draw(arg_keys[0], (DEVICES_ALL * SA, BS, BS), 1.0, 6.0, ((0, 256),))
    a_where = draw_a_where(jax.random.fold_in(arg_keys[4], 71), 0)
    b_blocks = bell_draw(arg_keys[2], (DEVICES_ALL * SB, BS, BS), (2 * BS) ** -0.5, 0.375, ((0, 256),))
    b_where = draw_b_where(jax.random.fold_in(arg_keys[4], 71), 0)
    return dict(a_blocks=a_blocks, a_where=a_where, b_blocks=b_blocks, b_where=b_where)


def pack_columns(blocks, where, total_k):
    target = jnp.where(where[:, 1] < CS, where[:, 0] * CS + where[:, 1], total_k * CS).astype(jnp.int32)
    flat = jax.ops.segment_sum(blocks.astype(jnp.float32), target, num_segments=total_k * CS + 1)[:total_k * CS]
    flat = flat.reshape(total_k, CS, BS, BS).transpose(0, 2, 1, 3)
    return flat.reshape(total_k, BS, CS * BS)


def reference(a_blocks, a_where, b_blocks, b_where):
    total_k = KD * N_COL * N_LAYER
    groups = N_COL * N_LAYER
    panel_a = a_blocks.reshape(N_ROW, groups * SA, BS, BS)
    panel_where = a_where.reshape(N_ROW, groups * SA, 2)
    cols_b = b_blocks.reshape(N_ROW, groups, SB, BS, BS).transpose(1, 0, 2, 3, 4).reshape(groups, N_ROW * SB, BS, BS)
    cols_where = b_where.reshape(N_ROW, groups, SB, 2).transpose(1, 0, 2, 3).reshape(groups, N_ROW * SB, 2)

    def make_dense(pair):
        return pack_columns(pair[0], pair[1], total_k)

    denses = lax.map(make_dense, (cols_b, cols_where))

    def row_tile(pair):
        blocks, where = pair
        blocks32 = blocks.astype(jnp.float32)

        def col_tile(dense):
            strips = jnp.take(dense, where[:, 1], axis=0)
            prod = jnp.einsum('gab,gbc->gac', blocks32, strips)
            placed = jax.ops.segment_sum(prod, where[:, 0], num_segments=RB + 1)[:RB]
            return placed.reshape(RB * BS, CS * BS)

        return lax.map(col_tile, denses)

    tiles = lax.map(row_tile, (panel_a, panel_where))
    return tiles.transpose(0, 2, 1, 3).reshape(N_ROW * RB * BS, groups * CS * BS)
```

```python
import jax
import jax.numpy as jnp
import numpy as np
from jax import lax
from jax.experimental import pallas as pl
from jax.experimental.pallas import tpu as pltpu
from jax.sharding import PartitionSpec as P

BS = 128
RB = 16
CS = 4
SA = 6
SB = 8
NZ = 8
NX = 4
NY = 4
INFO = 16
CUT = 448
UR = INFO + CUT
VR = SA * BS - CUT
BR = INFO + SB * BS
CHUNKS = NZ * NX
PARTS = NY * 2
GROUP = 8
LIST = CHUNKS * SA * CS + 2 * GROUP
KMAX = 64

Z_ORDER = (0, 1, -1, 2, -2, 3, -3, 4)
X_ORDER = (0, 1, -1, 2)
U_ORDER = [(dz, dx) for dx in X_ORDER for dz in Z_ORDER]
V_ORDER = [(dz, dx) for dz in Z_ORDER for dx in X_ORDER]


def cat(pieces):
    return jnp.concatenate(pieces, axis=0)


def tie(*arrays):
    return lax.optimization_barrier(arrays)


def along_z(x, d):
    return lax.ppermute(x, "col", [(i, (i + d) % NZ) for i in range(NZ)])


def along_x(x, d):
    return lax.ppermute(x, "layer", [(i, (i + d) % NX) for i in range(NX)])


def along_y(x, d):
    n = 2 * NY
    return lax.ppermute(x, "row", [(i, (i + 2 * d) % n) for i in range(n)])


def other_core(x):
    return lax.ppermute(x, "row", [(i, i ^ 1) for i in range(2 * NY)])


def with_info(first, second, blocks):
    n = first.shape[0]
    row = jnp.concatenate([first, second]).astype(jnp.bfloat16)
    tile = jnp.zeros((INFO, BS), jnp.bfloat16).at[0, : 2 * n].set(row)
    return cat([tile, blocks])


def kernel(tab, a_ref, b_ref, o_hbm, out, mid, bslot, work, work_mid, info, sinfo, sem):
    for i in range(CHUNKS):
        info[i : i + 1, :] = a_ref[i * UR : i * UR + INFO, :][0:1].astype(jnp.float32).astype(jnp.int32)
    for i in range(PARTS):
        info[CHUNKS + i : CHUNKS + i + 1, :] = (
            b_ref[i * BR : i * BR + INFO, :][0:1].astype(jnp.float32).astype(jnp.int32)
        )
    to_scalar = pltpu.make_async_copy(info, sinfo, sem.at[0])
    to_scalar.start()

    def clear(i, carry):
        out[i] = jnp.zeros((BS, CS * BS), jnp.float32)
        return carry

    lax.fori_loop(0, RB + 1, clear, 0)

    def join(i, carry):
        top = pl.multiple_of(i * UR + INFO + CUT // BS * BS, 16)
        low = pl.multiple_of(tab[1, i], 16)
        mid[pl.ds(pl.multiple_of(i * BS, BS), CUT % BS), :] = a_ref[pl.ds(top, CUT % BS), :]
        mid[pl.ds(pl.multiple_of(i * BS + CUT % BS, 16), BS - CUT % BS), :] = a_ref[pl.ds(low, BS - CUT % BS), :]
        return carry

    lax.fori_loop(0, CHUNKS, join, 0)

    def no_block(i, carry):
        bslot[i] = 0
        return carry

    lax.fori_loop(0, KMAX * CS, no_block, 0, unroll=8)
    to_scalar.wait()

    def place(i, carry):
        for s in range(SB):
            k = sinfo[CHUNKS + i, s]
            j = sinfo[CHUNKS + i, SB + s]

            @pl.when(j < CS)
            def _():
                bslot[k * CS + j] = (1 << 29) + (i * (BR // 16) + (INFO + s * BS) // 16) * 4 + j

        return carry

    lax.fori_loop(0, PARTS, place, 0)

    def listed(i, carry):
        n, n_mid = carry
        c = tab[0, i]
        low = tab[1, i] // 16
        for s in range(SA):
            r = sinfo[i, s]
            k = sinfo[i, SA + s] * CHUNKS + c
            live = (r < RB).astype(jnp.int32)
            if s < CUT // BS:
                row = i * (UR // 16) + (INFO + s * BS) // 16
            elif s == CUT // BS:
                row = i * (BS // 16)
            else:
                row = low + (s * BS - CUT) // 16
            word = row * (1 << 17) + r * (1 << 12)
            for j in range(CS):
                e = bslot[k * CS + j]
                there = (e >> 29) & live
                if s == CUT // BS:
                    work_mid[n_mid] = word + (e & 0xFFF)
                    n_mid = n_mid + there
                else:
                    work[n] = word + (e & 0xFFF)
                    n = n + there
        return n, n_mid

    n, n_mid = lax.fori_loop(0, CHUNKS, listed, (jnp.int32(0), jnp.int32(0)))
    for g in range(GROUP):
        work[n + g] = RB << 12
        work_mid[n_mid + g] = RB << 12

    def products(words, rows, count):
        def step(i, carry):
            results = []
            for g in range(GROUP):
                w = words[i * GROUP + g]
                a = rows[pl.ds(pl.multiple_of((w >> 17) * 16, 16), BS), :]
                b = b_ref[pl.ds(pl.multiple_of(((w >> 2) & 0x3FF) * 16, 16), BS), :]
                results.append(jnp.dot(a, b, preferred_element_type=jnp.float32))
            for g in range(GROUP):
                w = words[i * GROUP + g]
                out[(w >> 12) & 31, :, pl.ds(pl.multiple_of((w & 3) * BS, BS), BS)] += results[g]
            return carry

        lax.fori_loop(0, (count + GROUP - 1) // GROUP, step, 0)

    products(work, a_ref, n)
    products(work_mid, mid, n_mid)
    done = pltpu.make_async_copy(out.at[pl.ds(0, RB)], o_hbm, sem.at[1])
    done.start()
    done.wait()


def multiply(tab, a_all, b_all):
    vmem = pl.BlockSpec(memory_space=pltpu.VMEM)
    return pl.pallas_call(
        kernel,
        out_shape=jax.ShapeDtypeStruct((RB, BS, CS * BS), jnp.float32),
        in_specs=[pl.BlockSpec(memory_space=pltpu.SMEM), vmem, vmem],
        out_specs=pl.BlockSpec(memory_space=pl.ANY),
        scratch_shapes=[
            pltpu.VMEM((RB + 1, BS, CS * BS), jnp.float32),
            pltpu.VMEM((CHUNKS * BS, BS), jnp.bfloat16),
            pltpu.SMEM((KMAX * CS,), jnp.int32),
            pltpu.SMEM((LIST,), jnp.int32),
            pltpu.SMEM((LIST,), jnp.int32),
            pltpu.VMEM((CHUNKS + PARTS, BS), jnp.int32),
            pltpu.SMEM((CHUNKS + PARTS, BS), jnp.int32),
            pltpu.SemaphoreType.DMA((2,)),
        ],
        compiler_params=pltpu.CompilerParams(vmem_limit_bytes=40 * 2**20),
        cost_estimate=pl.CostEstimate(flops=10**9, bytes_accessed=13 * 10**6, transcendentals=0),
    )(tab, a_all, b_all)


def body(a_blocks, a_where, b_blocks, b_where):
    rows = a_blocks.reshape(SA * BS, BS)
    u = with_info(a_where[:, 0], a_where[:, 1] // CHUNKS, rows[:CUT])
    v = rows[CUT:]
    b = with_info(b_where[:, 0], b_where[:, 1], b_blocks.reshape(SB * BS, BS))

    u1, um1 = along_z(u, -1), along_z(u, 1)
    v1, vm1 = along_x(v, -1), along_x(v, 1)
    u2, um2 = along_z(u1, -1), along_z(um1, 1)
    v2 = along_x(v1, -1)
    u3, um3 = along_z(u2, -1), along_z(um2, 1)
    w = cat([v, v1, vm1, v2])
    w, u3, um3 = tie(w, u3, um3)
    u4 = along_z(u3, -1)
    w1, wm1 = along_z(w, -1), along_z(w, 1)
    x = cat([u, u1, um1, u2, um2, u3, um3, u4])
    x, b = tie(x, b)
    xp, xm = along_x(x, -1), along_x(x, 1)
    by1 = along_y(b, -1)
    w1, wm1, by1, b = tie(w1, wm1, by1, b)
    w2, wm2 = along_z(w1, -1), along_z(wm1, 1)
    bm1 = along_y(b, 1)
    w2, wm2, xp, xm, bm1, by1 = tie(w2, wm2, xp, xm, bm1, by1)
    half = NZ // 2 * UR
    xh0, xh1 = along_x(xp[:half], -1), along_x(xm[half:], 1)
    w3, wm3 = along_z(w2, -1), along_z(wm2, 1)
    by2 = along_y(by1, -1)
    w3, wm3, by2 = tie(w3, wm3, by2)
    mine = cat([b, by1, bm1, by2])
    other = other_core(mine)
    half = NX // 2 * VR
    wh0, wh1 = along_z(w3[:half], -1), along_z(wm3[half:], 1)

    a_all = cat([x, xp, xm, xh0, xh1, w, w1, wm1, w2, wm2, w3, wm3, wh0, wh1])
    b_all = cat([mine, other])

    u_order, v_order = np.array(U_ORDER), np.array(V_ORDER)
    place = {(dz % NZ, dx % NX): i for i, (dz, dx) in enumerate(V_ORDER)}
    v_row = [CHUNKS * UR + place[dz % NZ, dx % NX] * VR for dz, dx in U_ORDER]
    chunk = (lax.axis_index("col") + u_order[:, 0]) % NZ * NX + (lax.axis_index("layer") + u_order[:, 1]) % NX
    tab = jnp.stack([chunk.astype(jnp.int32), jnp.array(v_row, jnp.int32)])
    return multiply(tab, a_all, b_all).reshape(RB * BS, CS * BS)


def solution(mesh):
    in_specs = (
        P(("row", "col", "layer"), None, None),
        P(("row", "col", "layer"), None),
        P(("row", "col", "layer"), None, None),
        P(("row", "col", "layer"), None),
    )
    out_specs = P("row", ("col", "layer"))
    return jax.shard_map(body, mesh=mesh, in_specs=in_specs, out_specs=out_specs, check_vma=False)
```

```python
import functools

import jax
import jax.numpy as jnp
from jax import lax
from jax.experimental import pallas as pl
from jax.experimental.pallas import tpu as pltpu
from jax.sharding import PartitionSpec as P

BS = 128
RB = 16
CS = 4
SA = 6
SB = 8
NZ = 8
NX = 4
NY = 4
INFO = 16
CUT = 512
UR = INFO + CUT
VR = SA * BS - CUT
BR = INFO + SB * BS
CHUNKS = NZ * NX
PARTS = NY * 2
GROUP = 16
LIST = CHUNKS * SA * CS + 2 * GROUP

Z_ORDER = (0, 1, -1, 2, -2, 3, -3, 4)
X_ORDER = (0, 1, -1, 2)
U_ORDER = [(dz, dx) for dx in X_ORDER for dz in Z_ORDER]
V_ORDER = [(dz, dx) for dz in Z_ORDER for dx in X_ORDER]


def cat(pieces):
    return jnp.concatenate(pieces, axis=0)


def after(x, *others):
    return lax.optimization_barrier((x, *others))[0]


def along_z(x, d):
    return lax.ppermute(x, "col", [(i, (i + d) % NZ) for i in range(NZ)])


def along_x(x, d):
    return lax.ppermute(x, "layer", [(i, (i + d) % NX) for i in range(NX)])


def along_y(x, d):
    n = 2 * NY
    return lax.ppermute(x, "row", [(i, (i + 2 * d) % n) for i in range(n)])


def other_core(x):
    return lax.ppermute(x, "row", [(i, i ^ 1) for i in range(2 * NY)])


def with_info(where, blocks):
    tile = jnp.pad(where.T.astype(jnp.bfloat16), ((0, INFO - 2), (0, BS - where.shape[0])))
    return cat([tile, blocks])


def kernel(n_a, *refs):
    a_parts, refs = refs[:n_a], refs[n_a:]
    b_parts, refs = refs[:-11], refs[-11:]
    o_hbm, out, a_ref, b_ref, u_at, v_at, live, work, info, sinfo, sem = refs
    loads = []
    for slot, (parts, whole) in enumerate(((b_parts, b_ref), (a_parts, a_ref))):
        row = 0
        for part in parts:
            rows = part.shape[0]
            loads.append(pltpu.make_async_copy(part, whole.at[pl.ds(row, rows)], sem.at[slot]))
            row += rows
    for load in loads:
        load.start()

    q, t = lax.axis_index("col"), lax.axis_index("layer")
    for order, at, step, base in ((U_ORDER, u_at, 1, 0), (V_ORDER, v_at, VR // 16, CHUNKS * UR // 16)):
        for i, (dz, dx) in enumerate(order):
            at[((q + dz) & (NZ - 1)) * NX + ((t + dx) & (NX - 1))] = base + i * step

    def clear(i, carry):
        out[i] = jnp.zeros((BS, CS * BS), jnp.float32)
        return carry

    lax.fori_loop(0, RB + 1, clear, 0)
    for load in loads:
        load.wait()

    starts = [(a_ref, i * UR) for i in range(CHUNKS)] + [(b_ref, i * BR) for i in range(PARTS)]
    for i, (ref, at) in enumerate(starts):
        tile = ref[at : at + INFO, :].astype(jnp.float32)
        info[i : i + 1, :] = (tile[0:1] * 64 + tile[1:2]).astype(jnp.int32)
    to_scalar = pltpu.make_async_copy(info, sinfo, sem.at[2])
    to_scalar.start()
    to_scalar.wait()

    def found(i, n):
        for s in range(SB):
            v = sinfo[CHUNKS + i, s]
            live[n] = ((v >> 6) << 12) + (i * (BR // 16) + (INFO + s * BS) // 16) * 4 + (v & 3)
            n = n + jnp.where((v & 63) < CS, 1, 0)
        return n

    def listed(i, n):
        b = live[i]
        k, b = b >> 12, b & 0xFFF
        piece, low = u_at[k & (CHUNKS - 1)], v_at[k & (CHUNKS - 1)]
        top = ((piece * (UR // 16) + INFO // 16) << 17) + b
        low = (low << 17) + b
        for s in range(SA):
            x = sinfo[piece, s] ^ k
            work[n] = (top + (s * BS << 13) if s * BS < CUT else low + (s * BS - CUT << 13)) + (x << 6)
            n = n + jnp.where((x & ~((RB - 1) << 6)) == 0, 1, 0)
        return n

    n = lax.fori_loop(0, lax.fori_loop(0, PARTS, found, jnp.int32(0)), listed, jnp.int32(0))
    for g in range(GROUP):
        work[n + g] = RB << 12

    def products(i, carry):
        words = [work[i * GROUP + g] for g in range(GROUP)]
        results = []
        for w in words:
            a = a_ref[pl.ds(pl.multiple_of((w >> 17) * 16, 16), BS), :]
            b = b_ref[pl.ds(pl.multiple_of(((w >> 2) & 0x3FF) * 16, 16), BS), :]
            results.append(jnp.dot(a, b, preferred_element_type=jnp.float32))
        for w, result in zip(words, results):
            out[(w >> 12) & 31, :, pl.ds(pl.multiple_of((w & 3) * BS, BS), BS)] += result
        return carry

    lax.fori_loop(0, (n + GROUP - 1) // GROUP, products, 0)
    stores = [
        pltpu.make_async_copy(out.at[pl.ds(r, 4)], o_hbm.at[pl.ds(r, 4)], sem.at[3]) for r in range(0, RB, 4)
    ]
    for store in stores:
        store.start()
    for store in stores:
        store.wait()


def multiply(a_parts, b_parts):
    hbm = pl.BlockSpec(memory_space=pl.ANY)
    return pl.pallas_call(
        functools.partial(kernel, len(a_parts)),
        out_shape=jax.ShapeDtypeStruct((RB, BS, CS * BS), jnp.float32),
        in_specs=[hbm] * (len(a_parts) + len(b_parts)),
        out_specs=hbm,
        scratch_shapes=[
            pltpu.VMEM((RB + 1, BS, CS * BS), jnp.float32),
            pltpu.VMEM((CHUNKS * (UR + VR), BS), jnp.bfloat16),
            pltpu.VMEM((PARTS * BR, BS), jnp.bfloat16),
            pltpu.SMEM((CHUNKS,), jnp.int32),
            pltpu.SMEM((CHUNKS,), jnp.int32),
            pltpu.SMEM((PARTS * SB + 1,), jnp.int32),
            pltpu.SMEM((LIST,), jnp.int32),
            pltpu.VMEM((CHUNKS + PARTS, BS), jnp.int32),
            pltpu.SMEM((CHUNKS + PARTS, BS), jnp.int32),
            pltpu.SemaphoreType.DMA((4,)),
        ],
        compiler_params=pltpu.CompilerParams(vmem_limit_bytes=20 * 2**20),
        cost_estimate=pl.CostEstimate(flops=10**9, bytes_accessed=13 * 10**6, transcendentals=0),
    )(*a_parts, *b_parts)


def body(a_blocks, a_where, b_blocks, b_where):
    rows = a_blocks.reshape(SA * BS, BS)
    u = with_info(a_where, rows[:CUT])
    b = with_info(b_where, b_blocks.reshape(SB * BS, BS))
    u1, um1 = along_z(u, -1), along_z(u, 1)
    b = cat([b, other_core(b)])
    v = after(rows[CUT:], b)

    v1, vm1 = along_x(v, -1), along_x(v, 1)
    u2, um2 = along_z(u1, -1), along_z(um1, 1)
    by1 = along_y(after(b, u1), -1)
    v2 = along_x(v1, -1)
    u3, um3 = along_z(u2, -1), along_z(um2, 1)
    bm1 = along_y(after(b, u2), 1)
    w = after(cat([v, v1, vm1, v2]), u3, um3)
    u4 = along_z(u3, -1)
    w1, wm1 = along_z(w, -1), along_z(w, 1)
    x = cat([u, u1, um1, u2, um2, u3, um3, u4])
    xp, xm = along_x(x, -1), along_x(x, 1)
    w2, wm2 = along_z(w1, -1), along_z(wm1, 1)
    by2 = along_y(after(by1, w1), -1)
    w3, wm3 = along_z(w2, -1), along_z(wm2, 1)
    half = NZ // 2 * UR
    xh0, xh1 = along_x(after(xp, w3)[:half], -1), along_x(after(xm, wm3)[half:], 1)
    half = NX // 2 * VR
    wh0, wh1 = along_z(w3[:half], -1), along_z(wm3[half:], 1)

    a_parts = [x, xp, xm, xh0, xh1, w, w1, wm1, w2, wm2, w3, wm3, wh0, wh1]
    return multiply(a_parts, [b, by1, bm1, by2]).reshape(RB * BS, CS * BS)


def solution(mesh):
    in_specs = (
        P(("row", "col", "layer"), None, None),
        P(("row", "col", "layer"), None),
        P(("row", "col", "layer"), None, None),
        P(("row", "col", "layer"), None),
    )
    out_specs = P("row", ("col", "layer"))
    return jax.shard_map(body, mesh=mesh, in_specs=in_specs, out_specs=out_specs, check_vma=False)
```

```python
import functools

import jax
import jax.numpy as jnp
from jax import lax
from jax.experimental import pallas as pl
from jax.experimental.pallas import tpu as pltpu
from jax.sharding import PartitionSpec as P

BS = 128
RB = 16
CS = 4
SA = 6
SB = 8
NZ = 8
NX = 4
NY = 4
INFO = 16
CUT = 512
UR = INFO + CUT
VR = SA * BS - CUT
BR = INFO + SB * BS
CHUNKS = NZ * NX
PARTS = NY * 2
GROUP = 16
LIST = CHUNKS * SA * CS + 2 * GROUP

Z_ORDER = (0, 1, -1, 2, -2, 3, -3, 4)
X_ORDER = (0, 1, -1, 2)
U_ORDER = [(dz, dx) for dx in X_ORDER for dz in Z_ORDER]
V_ORDER = [(dz, dx) for dz in Z_ORDER for dx in X_ORDER]


def cat(pieces):
    return jnp.concatenate(pieces, axis=0)


def after(x, *others):
    return lax.optimization_barrier((x, *others))[0]


def along_z(x, d):
    return lax.ppermute(x, "col", [(i, (i + d) % NZ) for i in range(NZ)])


def along_x(x, d):
    return lax.ppermute(x, "layer", [(i, (i + d) % NX) for i in range(NX)])


def along_y(x, d):
    n = 2 * NY
    return lax.ppermute(x, "row", [(i, (i + 2 * d) % n) for i in range(n)])


def other_core(x):
    return lax.ppermute(x, "row", [(i, i ^ 1) for i in range(2 * NY)])


def with_info(where, blocks):
    tile = jnp.pad(where.T.astype(jnp.bfloat16), ((0, INFO - 2), (0, BS - where.shape[0])))
    return cat([tile, blocks])


def kernel(n_a, *refs):
    a_parts, refs = refs[:n_a], refs[n_a:]
    b_parts, refs = refs[:-12], refs[-12:]
    o_hbm, out, a_ref, b_ref, u_at, v_at, live, work, work_high, info, sinfo, sem = refs
    loads = []
    for slot, (parts, whole) in enumerate(((b_parts, b_ref), (a_parts, a_ref))):
        row = 0
        for part in parts:
            rows = part.shape[0]
            loads.append(pltpu.make_async_copy(part, whole.at[pl.ds(row, rows)], sem.at[slot]))
            row += rows
    for load in loads:
        load.start()

    q, t = lax.axis_index("col"), lax.axis_index("layer")
    for order, at, step, base in ((U_ORDER, u_at, 1, 0), (V_ORDER, v_at, VR // 16, CHUNKS * UR // 16)):
        for i, (dz, dx) in enumerate(order):
            at[((q + dz) & (NZ - 1)) * NX + ((t + dx) & (NX - 1))] = base + i * step

    def clear(i, carry):
        out[i] = jnp.zeros((BS, CS * BS), jnp.float32)
        return carry

    lax.fori_loop(0, RB // 2, clear, 0)
    for load in loads:
        load.wait()

    starts = [(a_ref, i * UR) for i in range(CHUNKS)] + [(b_ref, i * BR) for i in range(PARTS)]
    for i, (ref, at) in enumerate(starts):
        tile = ref[at : at + INFO, :].astype(jnp.float32)
        info[i : i + 1, :] = (tile[0:1] * 64 + tile[1:2]).astype(jnp.int32)
    to_scalar = pltpu.make_async_copy(info, sinfo, sem.at[2])
    to_scalar.start()
    lax.fori_loop(RB // 2, RB + 1, clear, 0)
    to_scalar.wait()

    def found(i, n):
        for s in range(SB):
            v = sinfo[CHUNKS + i, s]
            live[n] = ((v >> 6) << 12) + (i * (BR // 16) + (INFO + s * BS) // 16) * 4 + (v & 3)
            n = n + jnp.where((v & 63) < CS, 1, 0)
        return n

    def listed(i, carry):
        n, n_high = carry
        b = live[i]
        k, b = b >> 12, b & 0xFFF
        piece, low = u_at[k & (CHUNKS - 1)], v_at[k & (CHUNKS - 1)]
        top = ((piece * (UR // 16) + INFO // 16) << 17) + b
        low = (low << 17) + b
        for s in range(SA):
            x = sinfo[piece, s] ^ k
            word = (top + (s * BS << 13) if s * BS < CUT else low + (s * BS - CUT << 13)) + (x << 6)
            work[n] = word
            work_high[n_high] = word
            n = n + jnp.where((x & ~((RB // 2 - 1) << 6)) == 0, 1, 0)
            n_high = n_high + jnp.where(x - ((RB // 2) << 6) == (x & ((RB // 2 - 1) << 6)), 1, 0)
        return n, n_high

    count = lax.fori_loop(0, PARTS, found, jnp.int32(0))
    n, n_high = lax.fori_loop(0, count, listed, (jnp.int32(0), jnp.int32(0)))
    for g in range(GROUP):
        work[n + g] = RB << 12
        work_high[n_high + g] = RB << 12

    def products(words, count):
        def step(i, carry):
            group = [words[i * GROUP + g] for g in range(GROUP)]
            results = []
            for w in group:
                a = a_ref[pl.ds(pl.multiple_of((w >> 17) * 16, 16), BS), :]
                b = b_ref[pl.ds(pl.multiple_of(((w >> 2) & 0x3FF) * 16, 16), BS), :]
                results.append(jnp.dot(a, b, preferred_element_type=jnp.float32))
            for w, result in zip(group, results):
                out[(w >> 12) & 31, :, pl.ds(pl.multiple_of((w & 3) * BS, BS), BS)] += result
            return carry

        lax.fori_loop(0, (count + GROUP - 1) // GROUP, step, 0)

    half = RB // 2
    stores = [
        pltpu.make_async_copy(out.at[pl.ds(r, half)], o_hbm.at[pl.ds(r, half)], sem.at[3 + i])
        for i, r in enumerate((0, half))
    ]
    products(work, n)
    stores[0].start()
    products(work_high, n_high)
    stores[1].start()
    for store in stores:
        store.wait()


def multiply(a_parts, b_parts):
    hbm = pl.BlockSpec(memory_space=pl.ANY)
    return pl.pallas_call(
        functools.partial(kernel, len(a_parts)),
        out_shape=jax.ShapeDtypeStruct((RB, BS, CS * BS), jnp.float32),
        in_specs=[hbm] * (len(a_parts) + len(b_parts)),
        out_specs=hbm,
        scratch_shapes=[
            pltpu.VMEM((RB + 1, BS, CS * BS), jnp.float32),
            pltpu.VMEM((CHUNKS * (UR + VR), BS), jnp.bfloat16),
            pltpu.VMEM((PARTS * BR, BS), jnp.bfloat16),
            pltpu.SMEM((CHUNKS,), jnp.int32),
            pltpu.SMEM((CHUNKS,), jnp.int32),
            pltpu.SMEM((PARTS * SB + 1,), jnp.int32),
            pltpu.SMEM((LIST,), jnp.int32),
            pltpu.SMEM((LIST,), jnp.int32),
            pltpu.VMEM((CHUNKS + PARTS, BS), jnp.int32),
            pltpu.SMEM((CHUNKS + PARTS, BS), jnp.int32),
            pltpu.SemaphoreType.DMA((5,)),
        ],
        compiler_params=pltpu.CompilerParams(vmem_limit_bytes=20 * 2**20),
        cost_estimate=pl.CostEstimate(flops=10**9, bytes_accessed=13 * 10**6, transcendentals=0),
    )(*a_parts, *b_parts)


def body(a_blocks, a_where, b_blocks, b_where):
    rows = a_blocks.reshape(SA * BS, BS)
    u = with_info(a_where, rows[:CUT])
    b = with_info(b_where, b_blocks.reshape(SB * BS, BS))
    u1, um1 = along_z(u, -1), along_z(u, 1)
    b = cat([b, other_core(b)])
    v = after(rows[CUT:], b)

    v1, vm1 = along_x(v, -1), along_x(v, 1)
    u2, um2 = along_z(u1, -1), along_z(um1, 1)
    by1 = along_y(after(b, u1), -1)
    v2 = along_x(v1, -1)
    u3, um3 = along_z(after(u2, v1), -1), along_z(after(um2, vm1), 1)
    w = after(cat([v, v1, vm1, v2]), u3, um3)
    u4 = along_z(u3, -1)
    bm1 = along_y(after(b, u4), 1)
    w1, wm1 = along_z(w, -1), along_z(w, 1)
    x = after(cat([u, u1, um1, u2, um2, u3, um3, u4]), v2, by1)
    xp, xm = along_x(x, -1), along_x(x, 1)
    w2, wm2 = along_z(w1, -1), along_z(wm1, 1)
    by2 = along_y(after(by1, w1), -1)
    w3, wm3 = along_z(w2, -1), along_z(wm2, 1)
    half = NZ // 2 * UR
    xh0, xh1 = along_x(after(xp, w3)[:half], -1), along_x(after(xm, wm3)[half:], 1)
    half = NX // 2 * VR
    wh0, wh1 = along_z(after(w3, bm1)[:half], -1), along_z(after(wm3, bm1)[half:], 1)

    a_parts = [x, xp, xm, xh0, xh1, w, w1, wm1, w2, wm2, w3, wm3, wh0, wh1]
    return multiply(a_parts, [b, by1, bm1, by2]).reshape(RB * BS, CS * BS)


def solution(mesh):
    in_specs = (
        P(("row", "col", "layer"), None, None),
        P(("row", "col", "layer"), None),
        P(("row", "col", "layer"), None, None),
        P(("row", "col", "layer"), None),
    )
    out_specs = P("row", ("col", "layer"))
    return jax.shard_map(body, mesh=mesh, in_specs=in_specs, out_specs=out_specs, check_vma=False)
```
